32 devices in a mesh: dp: 2 (over x), cent: 16 (over z, y, core).
Axes of the slice: x: 2, y: 2, z: 4, core: 2. Of those that a mesh axis runs over, the one named last changes fastest.
Arguments:
- points: bfloat16 [1536, 1024], P(('dp', 'cent')), may hold values from -6 to 6
- assign: int32 [1536], P(('dp', 'cent')), may hold values from 0 to 8191, as said below
- centroids: float32 [8192, 1024], P('cent'), may hold values from -6 to 6
- counts: int32 [8192], P('cent'), may hold values from 1 to 4
Outputs:
- new_centroids: float32 [8192, 1024], P('cent')
- best: float32 [1536], P(('dp', 'cent'))
The draws below stay inside these ranges and needn't reach their ends.
Inputs may be any that keep to these rules, and one draw needn't show every extreme that they name: `assign`: split the points into aligned blocks of 768 points in order (the points of one dp index). In every block, the clusters k * 512 to (k + 1) * 512 - 1 receive exactly 48 points together, for every k.
All inputs are finite; a program needn't handle non-finite values.
Results may differ from the reference program's by a relative error of at most 0.0003.
Values may be sent and summed in bfloat16 or wider, within the bound.
A program may use at most 128 MiB of HBM per device.

```python
import jax
import jax.numpy as jnp
from jax import lax

D = 1024
K_DEV = 512
P_DEV = 48
K = 8192
N = 1536
N_CENT = 16


def draw_assign(key, part):
    shards = K // K_DEV
    group = P_DEV * shards
    blocks = N // group
    keys = jax.random.split(jax.random.fold_in(key, 17), blocks)

    def one_block(block_key):
        first, second = jax.random.split(block_key)
        order = jax.random.permutation(first, group).astype(jnp.int32)
        shard = order % shards
        within = jax.random.randint(second, (group,), 0, K_DEV, dtype=jnp.int32)
        return shard * K_DEV + within
    return jax.vmap(one_block)(keys).reshape(N).astype(jnp.int32)


def place_ends(drawn, key, low, high):
    dims = drawn.shape
    index_at = [jax.random.randint(jax.random.fold_in(key, axis), (), 0, dims[axis]) for axis in range(len(dims))]
    drawn = drawn.at[tuple(index_at)].set(low)
    longest = dims.index(max(dims))
    index_at[longest] = (index_at[longest] + 1) % dims[longest]
    return drawn.at[tuple(index_at)].set(high)


def level_of(key, extent, cuts, least, top_value):
    def one(axis_at, parts):
        draws = jax.random.uniform(jax.random.fold_in(jax.random.fold_in(key, 6), axis_at), (parts,), jnp.float32, least / len(cuts), top_value / len(cuts))
        return jnp.repeat(jnp.exp(draws), extent[axis_at] // parts).reshape((-1,) + (1,) * (len(extent) - axis_at - 1))

    factor_of = one(*cuts[0])
    for cut in cuts[1:]:
        factor_of = factor_of * one(*cut)
    return factor_of


def scatter_about(rng, extent, width, most, pieces=(), kind=jnp.bfloat16):
    level = level_of(rng, extent, pieces, -0.22, 0.18) if pieces else 1.0
    entries = jax.random.normal(rng, extent, jnp.float32) * width * level
    return jnp.minimum(jnp.maximum(entries, -most), most).astype(kind)


def setup_inputs(seed: int = 0) -> dict:
    key_of = jax.random.split(jax.random.key(seed), 5)
    return {
        "points": scatter_about(key_of[0], (N, D), 1.0, 6.0, ((0, 32),)),
        "assign": draw_assign(jax.random.fold_in(key_of[4], 71), 0),
        "centroids": scatter_about(key_of[2], (K, D), 1.0, 6.0, ((0, 16),), jnp.float32),
        "counts": place_ends(jax.random.randint(key_of[3], (K,), 1, 5), jax.random.fold_in(key_of[3], 1), 1, 4).astype(jnp.int32),
    }


def reference(points, assign, centroids, counts):
    values = points.astype(jnp.float32)
    sums = jax.ops.segment_sum(values, assign, num_segments=K_DEV * N_CENT)
    merged = centroids * counts.astype(jnp.float32)[:, None] + sums
    fresh = merged * lax.rsqrt(lax.optimization_barrier(jnp.mean(merged * merged, axis=1, keepdims=True)) + 1e-05)
    rounded = lax.optimization_barrier(fresh.astype(jnp.bfloat16)).astype(jnp.float32)
    blocks = rounded.reshape(N_CENT, K_DEV, D)

    def block_best(block):
        return lax.optimization_barrier(jnp.max(jnp.dot(values, block.T, preferred_element_type=jnp.float32), axis=1))
    top = lax.optimization_barrier(jnp.max(lax.map(block_best, blocks), axis=0))
    scale = D * jnp.sqrt(lax.optimization_barrier(jnp.mean(values * values, axis=1)) + 1e-06)
    return (fresh, top / scale)
```

```python
import functools

import jax
import jax.numpy as jnp
from jax import lax
from jax.experimental import pallas as pl
from jax.experimental.pallas import tpu as pltpu
from jax.sharding import PartitionSpec as P

F32 = jnp.float32
BF16 = jnp.bfloat16
LANES = 128
CHUNK = 128


def dot_nt(a, b):
    return lax.dot_general(a, b, (((1,), (1,)), ((), ())), preferred_element_type=F32)


def iota(shape, dim):
    return lax.broadcasted_iota(jnp.int32, shape, dim)


def remote(src, dst, send, recv, where):
    return pltpu.make_async_remote_copy(
        src_ref=src, dst_ref=dst, send_sem=send, recv_sem=recv,
        device_id=where, device_id_type=pl.DeviceIdType.MESH)


def kernel(ndp, ncent, wa, points_ref, assign_ref, cent_ref, counts_ref,
           fresh_ref, best_ref,
           pts, labs, keys, acc, sel, sellab, merged, rounded, outbest, inbest,
           pts_send, pts_recv, lab_send, lab_recv, sel_send, sel_recv,
           sl_send, sl_recv, best_send, best_recv, loc):
    pdev, width = points_ref.shape
    kdev = cent_ref.shape[0]
    wide = sellab.shape[2]
    wb = ncent // (2 * wa)
    me = lax.axis_index("cent")
    mydp = lax.axis_index("dp")
    core = lax.rem(me, 2)
    b = lax.rem(me // 2, wb)
    a = me // (2 * wb)

    fetch = pltpu.make_async_copy(cent_ref, merged, loc.at[0])
    fetch.start()

    def block(s):
        return pts.at[pl.ds(pl.multiple_of(s * pdev, 16), pdev), :]

    own = pltpu.make_async_copy(points_ref, block(me), loc.at[1])
    own.start()

    barrier = pltpu.get_barrier_semaphore()
    for o in range(1, ncent):
        pl.semaphore_signal(barrier, inc=1, device_id={"cent": lax.rem(me + o, ncent)},
                            device_id_type=pl.DeviceIdType.MESH)
    for o in range(1, ndp):
        pl.semaphore_signal(barrier, inc=1, device_id={"dp": lax.rem(mydp + o, ndp)},
                            device_id_type=pl.DeviceIdType.MESH)
    labs[me] = jnp.full((1, LANES), -1, jnp.int32)
    labs[me, 0:1, 0:pdev] = assign_ref[...]
    own.wait()
    pl.semaphore_wait(barrier, ncent + ndp - 2)

    def index(a_, b_, c_):
        return (a_ * wb + b_) * 2 + c_

    if wa == 4:
        others = [a + 1 - 2 * lax.rem(a, 2), lax.rem(a + 2, 4), 3 - a]
    else:
        others = [lax.rem(a + o, wa) for o in range(1, wa)]
    bothers = [lax.rem(b + o, wb) for o in range(1, wb)]
    sent = []

    def send(s, to):
        i = len(sent)
        c = remote(block(s), block(s), pts_send.at[i], pts_recv.at[s], {"cent": to})
        c.start()
        sent.append(c)

    def arrive(s):
        remote(block(s), block(s), pts_send.at[0], pts_recv.at[s], {"cent": me}).wait_recv()

    for b_ in bothers:
        send(me, index(a, b_, core))
    for a_ in others:
        send(me, index(a_, b, core))
    send(me, index(a, b, 1 - core))
    labcopies = []
    for o in range(1, ncent):
        to = lax.rem(me + o, ncent)
        c = remote(labs.at[me], labs.at[me], lab_send.at[o], lab_recv.at[me], {"cent": to})
        c.start()
        labcopies.append(c)

    eye = iota((CHUNK, CHUNK), 0) == iota((CHUNK, CHUNK), 1)
    fetch.wait()
    for j in range(kdev // CHUNK):
        rows = pl.ds(j * CHUNK, CHUNK)
        line = counts_ref[:, j * CHUNK:(j + 1) * CHUNK].astype(F32)
        column = jnp.sum(jnp.where(eye, line, 0.0), axis=1, keepdims=True)
        merged[rows, :] = merged[rows, :] * column

    def forward(s):
        arrive(s)
        for b_ in bothers:
            send(s, index(a, b_, core))
        send(s, index(a, b, 1 - core))

    forward(index(others[0], b, core))

    for o in range(1, ncent):
        s = lax.rem(me + o, ncent)
        remote(labs.at[s], labs.at[s], lab_send.at[0], lab_recv.at[s], {"cent": me}).wait_recv()
    local = labs[...].reshape(ncent, LANES) - me * kdev
    mine = (local >= 0) & (local < kdev) & (iota((ncent, LANES), 1) < pdev)
    ones = jnp.where(mine, 1.0, 0.0).astype(BF16)
    upper = jnp.where(iota((LANES, LANES), 0) < iota((LANES, LANES), 1), 1.0, 0.0).astype(BF16)
    lower = jnp.where(iota((ncent, ncent), 1) < iota((ncent, ncent), 0), 1.0, 0.0).astype(BF16)
    within = jnp.dot(ones, upper, preferred_element_type=F32)
    before = jnp.sum(jnp.dot(lower, ones, preferred_element_type=F32), axis=1, keepdims=True)
    keys[...] = jnp.where(mine, within + before, -1.0)

    slot = iota((pdev, LANES), 0).astype(F32)
    localf = jnp.where(mine, local + 1, 0).astype(F32)
    keyv = keys[...]
    total = jnp.zeros((pdev, LANES), F32)
    for s in range(ncent):
        total += jnp.where(slot == keyv[s:s + 1, :], localf[s:s + 1, :], 0.0)
    labcol = jnp.sum(total, axis=1, keepdims=True)
    place = iota((pdev, wide), 1) == iota((pdev, wide), 0) + mydp * pdev
    sellab[mydp] = jnp.sum(jnp.where(place, labcol, 0.0), axis=0, keepdims=True)
    slcopies = []
    for o in range(1, ndp):
        to = lax.rem(mydp + o, ndp)
        c = remote(sellab.at[mydp], sellab.at[mydp], sl_send.at[o], sl_recv.at[mydp], {"dp": to})
        c.start()
        slcopies.append(c)
    if sel.shape[0] > ndp * pdev:
        sel[ndp * pdev:, :] = jnp.zeros((sel.shape[0] - ndp * pdev, width), BF16)

    for a_ in others[1:]:
        forward(index(a_, b, core))

    def pick(s):
        key = keys[pl.ds(s, 1), :]
        choose = jnp.where(slot == key, 1.0, 0.0).astype(BF16)[:, :pdev]
        return jnp.dot(choose, block(s)[...], preferred_element_type=F32)

    acc[...] = pick(me)
    for a_ in others:
        acc[...] += pick(index(a_, b, core))
    arrive(index(a, b, 1 - core))
    acc[...] += pick(index(a, b, 1 - core))
    for a_ in others:
        s = index(a_, b, 1 - core)
        arrive(s)
        acc[...] += pick(s)
    for a_ in [a] + others:
        for b_ in bothers:
            s = index(a_, b_, core)
            arrive(s)
            send(s, index(a, b, 1 - core))
            acc[...] += pick(s)
    for a_ in [a] + others:
        for b_ in bothers:
            s = index(a_, b_, 1 - core)
            arrive(s)
            acc[...] += pick(s)

    def selrows(d):
        return sel.at[pl.ds(pl.multiple_of(d * pdev, 16), pdev), :]

    selrows(mydp)[...] = acc[...].astype(BF16)
    selcopies = []
    for o in range(1, ndp):
        to = lax.rem(mydp + o, ndp)
        c = remote(selrows(mydp), selrows(mydp), sel_send.at[o], sel_recv.at[mydp], {"dp": to})
        c.start()
        selcopies.append(c)
    for o in range(1, ndp):
        d = lax.rem(mydp + o, ndp)
        remote(sellab.at[d], sellab.at[d], sl_send.at[0], sl_recv.at[d], {"dp": mydp}).wait_recv()
        remote(selrows(d), selrows(d), sel_send.at[0], sel_recv.at[d], {"dp": mydp}).wait_recv()

    labrow = jnp.sum(sellab[...].reshape(ndp, wide), axis=0, keepdims=True) - 1.0
    outs = []
    for j in range(kdev // CHUNK):
        rows = pl.ds(j * CHUNK, CHUNK)
        ids = (iota((CHUNK, wide), 0) + j * CHUNK).astype(F32)
        onehot = jnp.where(ids == labrow, 1.0, 0.0).astype(BF16)
        value = merged[rows, :] + jnp.dot(onehot, sel[...], preferred_element_type=F32)
        value = value * lax.rsqrt(jnp.mean(value * value, axis=1, keepdims=True) + 1e-05)
        merged[rows, :] = value
        c = pltpu.make_async_copy(merged.at[rows, :], fresh_ref.at[rows, :], loc.at[2 + j])
        c.start()
        outs.append(c)
        rounded[rows, :] = value.astype(BF16)

    npts = ncent * pdev
    step = 256 if npts % 256 == 0 else 128
    parts = []
    for t in range(npts // step):
        scores = dot_nt(rounded[...], pts[t * step:(t + 1) * step, :])
        parts.append(jnp.max(scores, axis=0, keepdims=True))
    line = jnp.concatenate(parts, axis=1)
    for s in range(ncent):
        turned = pltpu.roll(line, (npts - s * pdev) % npts, 1) if s else line
        outbest[s] = turned[:, :LANES]
    bestcopies = []
    for o in range(1, ncent):
        to = lax.rem(me + o, ncent)
        c = remote(outbest.at[to], inbest.at[me], best_send.at[o], best_recv.at[me], {"cent": to})
        c.start()
        bestcopies.append(c)
    inbest[me] = outbest[me]

    values = block(me)[...].astype(F32)
    square = jnp.mean(values * values, axis=1, keepdims=True)
    diag = iota((pdev, pdev), 0) == iota((pdev, pdev), 1)
    square = jnp.sum(jnp.where(diag, square, 0.0), axis=0, keepdims=True)
    scale = width * jnp.sqrt(square + 1e-06)

    for c in sent + labcopies + slcopies + selcopies:
        c.wait_send()
    for o in range(1, ncent):
        s = lax.rem(me + o, ncent)
        remote(outbest.at[s], inbest.at[s], best_send.at[0], best_recv.at[s], {"cent": me}).wait_recv()
    top = jnp.max(inbest[...].reshape(ncent, LANES), axis=0, keepdims=True)
    best_ref[...] = top[:, :pdev] / scale
    for c in bestcopies:
        c.wait_send()
    for c in outs:
        c.wait()


def per_device(ndp, ncent, points, assign, centroids, counts):
    kdev, width = centroids.shape
    pdev = points.shape[0]
    wa = 4
    wb = ncent // (2 * wa)
    wide = -(-ndp * pdev // LANES) * LANES
    nsend = (wa - 1) + (wb - 1) * wa + wa * wb
    vmem = pl.BlockSpec(memory_space=pltpu.VMEM)
    anyspace = pl.BlockSpec(memory_space=pl.ANY)
    dma = pltpu.SemaphoreType.DMA
    fresh, best = pl.pallas_call(
        functools.partial(kernel, ndp, ncent, wa),
        out_shape=(jax.ShapeDtypeStruct((kdev, width), F32), jax.ShapeDtypeStruct((1, pdev), F32)),
        in_specs=[anyspace, vmem, anyspace, vmem],
        out_specs=(anyspace, vmem),
        scratch_shapes=[
            pltpu.VMEM((ncent * pdev, width), BF16),
            pltpu.VMEM((ncent, 1, LANES), jnp.int32),
            pltpu.VMEM((ncent, LANES), F32),
            pltpu.VMEM((pdev, width), F32),
            pltpu.VMEM((wide, width), BF16),
            pltpu.VMEM((ndp, 1, wide), F32),
            pltpu.VMEM((kdev, width), F32),
            pltpu.VMEM((kdev, width), BF16),
            pltpu.VMEM((ncent, 1, LANES), F32),
            pltpu.VMEM((ncent, 1, LANES), F32),
            dma((nsend,)), dma((ncent,)), dma((ncent,)), dma((ncent,)),
            dma((ndp,)), dma((ndp,)), dma((ndp,)), dma((ndp,)),
            dma((ncent,)), dma((ncent,)), dma((2 + kdev // CHUNK,)),
        ],
        compiler_params=pltpu.CompilerParams(
            collective_id=0, has_side_effects=True, vmem_limit_bytes=32 * 2**20),
    )(points, assign.reshape(1, pdev), centroids, counts.reshape(1, kdev))
    return fresh, best.reshape(pdev)


def solution(mesh):
    placed = (P(("dp", "cent"), None), P(("dp", "cent")), P("cent", None), P("cent"))
    return jax.shard_map(
        functools.partial(per_device, mesh.shape["dp"], mesh.shape["cent"]),
        mesh=mesh,
        in_specs=placed,
        out_specs=(P("cent", None), P(("dp", "cent"))),
        check_vma=False,
    )
```

```python
import functools

import jax
import jax.numpy as jnp
from jax import lax
from jax.experimental import pallas as pl
from jax.experimental.pallas import tpu as pltpu
from jax.sharding import PartitionSpec as P

F32 = jnp.float32
BF16 = jnp.bfloat16
LANES = 128
CHUNK = 128


def dot_nt(a, b):
    return lax.dot_general(a, b, (((1,), (1,)), ((), ())), preferred_element_type=F32)


def iota(shape, dim):
    return lax.broadcasted_iota(jnp.int32, shape, dim)


def remote(src, dst, send, recv, where):
    return pltpu.make_async_remote_copy(
        src_ref=src, dst_ref=dst, send_sem=send, recv_sem=recv,
        device_id=where, device_id_type=pl.DeviceIdType.MESH)


def kernel(ndp, ncent, wa, points_ref, assign_ref, cent_ref, counts_ref,
           fresh_ref, best_ref,
           pts, labs, keys, acc, sel, sellab, merged, rounded, outbest, inbest,
           pts_send, pts_recv, lab_send, lab_recv, sel_send, sel_recv,
           sl_send, sl_recv, best_send, best_recv, loc):
    pdev, width = points_ref.shape
    kdev = cent_ref.shape[0]
    wide = sellab.shape[2]
    wb = ncent // (2 * wa)
    me = lax.axis_index("cent")
    mydp = lax.axis_index("dp")
    core = lax.rem(me, 2)
    b = lax.rem(me // 2, wb)
    a = me // (2 * wb)

    fetch = pltpu.make_async_copy(cent_ref, merged, loc.at[0])
    fetch.start()

    def block(s):
        return pts.at[pl.ds(pl.multiple_of(s * pdev, 16), pdev), :]

    own = pltpu.make_async_copy(points_ref, block(me), loc.at[1])
    own.start()

    barrier = pltpu.get_barrier_semaphore()
    for o in range(1, ncent):
        pl.semaphore_signal(barrier, inc=1, device_id={"cent": lax.rem(me + o, ncent)},
                            device_id_type=pl.DeviceIdType.MESH)
    for o in range(1, ndp):
        pl.semaphore_signal(barrier, inc=1, device_id={"dp": lax.rem(mydp + o, ndp)},
                            device_id_type=pl.DeviceIdType.MESH)
    labs[me] = jnp.full((1, LANES), -1, jnp.int32)
    labs[me, 0:1, 0:pdev] = assign_ref[...]
    own.wait()
    pl.semaphore_wait(barrier, ncent + ndp - 2)

    def index(a_, b_, c_):
        return (a_ * wb + b_) * 2 + c_

    if wa == 4:
        half = a // 2
        others = [1 - a + 4 * half, 2 - half, 3 - 3 * half]
    else:
        others = [lax.rem(a + o, wa) for o in range(1, wa)]
    bothers = [lax.rem(b + o, wb) for o in range(1, wb)]
    sent = []

    def send(s, to, when=None):
        i = len(sent)

        def copy():
            return remote(block(s), block(s), pts_send.at[i], pts_recv.at[s], {"cent": to})

        sent.append((when, copy))
        if when is None:
            copy().start()
        else:
            pl.when(when)(lambda: copy().start())

    def arrive(s):
        remote(block(s), block(s), pts_send.at[0], pts_recv.at[s], {"cent": me}).wait_recv()

    for b_ in bothers:
        send(me, index(a, b_, core))
    send(me, index(a - 1, b, core), a > 0)
    send(me, index(a + 1, b, core), a < wa - 1)
    send(me, index(a, b, 1 - core))
    labcopies = []
    for o in range(1, ncent):
        to = lax.rem(me + o, ncent)
        c = remote(labs.at[me], labs.at[me], lab_send.at[o], lab_recv.at[me], {"cent": to})
        c.start()
        labcopies.append(c)

    eye = iota((CHUNK, CHUNK), 0) == iota((CHUNK, CHUNK), 1)
    fetch.wait()
    for j in range(kdev // CHUNK):
        rows = pl.ds(j * CHUNK, CHUNK)
        line = counts_ref[:, j * CHUNK:(j + 1) * CHUNK].astype(F32)
        column = jnp.sum(jnp.where(eye, line, 0.0), axis=1, keepdims=True)
        merged[rows, :] = merged[rows, :] * column

    for k in range(1, wa):
        for way in (1, -1):
            origin = a + way * k
            valid = (origin < wa) if way > 0 else (origin >= 0)
            onward = (a > 0) if way > 0 else (a < wa - 1)
            s = index(origin, b, core)
            pl.when(valid)(lambda s=s: arrive(s))
            if k < wa - 1:
                send(s, index(a - way, b, core), valid & onward)
            for b_ in bothers:
                send(s, index(a, b_, core), valid)
            send(s, index(a, b, 1 - core), valid)

    for o in range(1, ncent):
        s = lax.rem(me + o, ncent)
        remote(labs.at[s], labs.at[s], lab_send.at[0], lab_recv.at[s], {"cent": me}).wait_recv()
    local = labs[...].reshape(ncent, LANES) - me * kdev
    mine = (local >= 0) & (local < kdev) & (iota((ncent, LANES), 1) < pdev)
    ones = jnp.where(mine, 1.0, 0.0).astype(BF16)
    upper = jnp.where(iota((LANES, LANES), 0) < iota((LANES, LANES), 1), 1.0, 0.0).astype(BF16)
    lower = jnp.where(iota((ncent, ncent), 1) < iota((ncent, ncent), 0), 1.0, 0.0).astype(BF16)
    within = jnp.dot(ones, upper, preferred_element_type=F32)
    before = jnp.sum(jnp.dot(lower, ones, preferred_element_type=F32), axis=1, keepdims=True)
    keys[...] = jnp.where(mine, within + before, -1.0)

    slot = iota((pdev, LANES), 0).astype(F32)
    localf = jnp.where(mine, local + 1, 0).astype(F32)
    keyv = keys[...]
    total = jnp.zeros((pdev, LANES), F32)
    for s in range(ncent):
        total += jnp.where(slot == keyv[s:s + 1, :], localf[s:s + 1, :], 0.0)
    labcol = jnp.sum(total, axis=1, keepdims=True)
    place = iota((pdev, wide), 1) == iota((pdev, wide), 0) + mydp * pdev
    sellab[mydp] = jnp.sum(jnp.where(place, labcol, 0.0), axis=0, keepdims=True)
    slcopies = []
    for o in range(1, ndp):
        to = lax.rem(mydp + o, ndp)
        c = remote(sellab.at[mydp], sellab.at[mydp], sl_send.at[o], sl_recv.at[mydp], {"dp": to})
        c.start()
        slcopies.append(c)
    if sel.shape[0] > ndp * pdev:
        sel[ndp * pdev:, :] = jnp.zeros((sel.shape[0] - ndp * pdev, width), BF16)

    def pick(s):
        key = keys[pl.ds(s, 1), :]
        choose = jnp.where(slot == key, 1.0, 0.0).astype(BF16)[:, :pdev]
        return jnp.dot(choose, block(s)[...], preferred_element_type=F32)

    acc[...] = pick(me)
    for a_ in others:
        acc[...] += pick(index(a_, b, core))
    arrive(index(a, b, 1 - core))
    acc[...] += pick(index(a, b, 1 - core))
    for a_ in others:
        s = index(a_, b, 1 - core)
        arrive(s)
        acc[...] += pick(s)
    for a_ in [a] + others:
        for b_ in bothers:
            s = index(a_, b_, core)
            arrive(s)
            send(s, index(a, b, 1 - core))
            acc[...] += pick(s)
    for a_ in [a] + others:
        for b_ in bothers:
            s = index(a_, b_, 1 - core)
            arrive(s)
            acc[...] += pick(s)

    def selrows(d):
        return sel.at[pl.ds(pl.multiple_of(d * pdev, 16), pdev), :]

    selrows(mydp)[...] = acc[...].astype(BF16)
    selcopies = []
    for o in range(1, ndp):
        to = lax.rem(mydp + o, ndp)
        c = remote(selrows(mydp), selrows(mydp), sel_send.at[o], sel_recv.at[mydp], {"dp": to})
        c.start()
        selcopies.append(c)
    for o in range(1, ndp):
        d = lax.rem(mydp + o, ndp)
        remote(sellab.at[d], sellab.at[d], sl_send.at[0], sl_recv.at[d], {"dp": mydp}).wait_recv()
        remote(selrows(d), selrows(d), sel_send.at[0], sel_recv.at[d], {"dp": mydp}).wait_recv()

    labrow = jnp.sum(sellab[...].reshape(ndp, wide), axis=0, keepdims=True) - 1.0
    for j in range(kdev // CHUNK):
        rows = pl.ds(j * CHUNK, CHUNK)
        ids = (iota((CHUNK, wide), 0) + j * CHUNK).astype(F32)
        onehot = jnp.where(ids == labrow, 1.0, 0.0).astype(BF16)
        value = merged[rows, :] + jnp.dot(onehot, sel[...], preferred_element_type=F32)
        value = value * lax.rsqrt(jnp.mean(value * value, axis=1, keepdims=True) + 1e-05)
        fresh_ref[rows, :] = value
        rounded[rows, :] = value.astype(BF16)

    npts = ncent * pdev
    step = 256 if npts % 256 == 0 else 128
    parts = []
    for t in range(npts // step):
        scores = dot_nt(rounded[...], pts[t * step:(t + 1) * step, :])
        parts.append(jnp.max(scores, axis=0, keepdims=True))
    line = jnp.concatenate(parts, axis=1)
    for s in range(ncent):
        turned = pltpu.roll(line, (npts - s * pdev) % npts, 1) if s else line
        outbest[s] = turned[:, :LANES]
    bestcopies = []
    for o in range(1, ncent):
        to = lax.rem(me + o, ncent)
        c = remote(outbest.at[to], inbest.at[me], best_send.at[o], best_recv.at[me], {"cent": to})
        c.start()
        bestcopies.append(c)
    inbest[me] = outbest[me]

    values = block(me)[...].astype(F32)
    square = jnp.mean(values * values, axis=1, keepdims=True)
    diag = iota((pdev, pdev), 0) == iota((pdev, pdev), 1)
    square = jnp.sum(jnp.where(diag, square, 0.0), axis=0, keepdims=True)
    scale = width * jnp.sqrt(square + 1e-06)

    for when, copy in sent:
        if when is None:
            copy().wait_send()
        else:
            pl.when(when)(lambda copy=copy: copy().wait_send())
    for c in labcopies + slcopies + selcopies:
        c.wait_send()
    for o in range(1, ncent):
        s = lax.rem(me + o, ncent)
        remote(outbest.at[s], inbest.at[s], best_send.at[0], best_recv.at[s], {"cent": me}).wait_recv()
    top = jnp.max(inbest[...].reshape(ncent, LANES), axis=0, keepdims=True)
    best_ref[...] = top[:, :pdev] / scale
    for c in bestcopies:
        c.wait_send()


def per_device(ndp, ncent, points, assign, centroids, counts):
    kdev, width = centroids.shape
    pdev = points.shape[0]
    wa = 4
    wb = ncent // (2 * wa)
    wide = -(-ndp * pdev // LANES) * LANES
    nsend = wb + 2 + 2 * (wa - 1) * (wb + 1) + wa * wb
    vmem = pl.BlockSpec(memory_space=pltpu.VMEM)
    hbm = pl.BlockSpec(memory_space=pltpu.MemorySpace.HBM)
    dma = pltpu.SemaphoreType.DMA
    fresh, best = pl.pallas_call(
        functools.partial(kernel, ndp, ncent, wa),
        out_shape=(pltpu.MemorySpace.VMEM((kdev, width), F32), jax.ShapeDtypeStruct((1, pdev), F32)),
        in_specs=[hbm, vmem, hbm, vmem],
        out_specs=(vmem, vmem),
        scratch_shapes=[
            pltpu.VMEM((ncent * pdev, width), BF16),
            pltpu.VMEM((ncent, 1, LANES), jnp.int32),
            pltpu.VMEM((ncent, LANES), F32),
            pltpu.VMEM((pdev, width), F32),
            pltpu.VMEM((wide, width), BF16),
            pltpu.VMEM((ndp, 1, wide), F32),
            pltpu.VMEM((kdev, width), F32),
            pltpu.VMEM((kdev, width), BF16),
            pltpu.VMEM((ncent, 1, LANES), F32),
            pltpu.VMEM((ncent, 1, LANES), F32),
            dma((nsend,)), dma((ncent,)), dma((ncent,)), dma((ncent,)),
            dma((ndp,)), dma((ndp,)), dma((ndp,)), dma((ndp,)),
            dma((ncent,)), dma((ncent,)), dma((2,)),
        ],
        compiler_params=pltpu.CompilerParams(
            collective_id=0, has_side_effects=True, vmem_limit_bytes=60 * 2**20),
    )(points, assign.reshape(1, pdev), centroids, counts.reshape(1, kdev))
    return fresh, best.reshape(pdev)


def solution(mesh):
    placed = (P(("dp", "cent"), None), P(("dp", "cent")), P("cent", None), P("cent"))
    return jax.shard_map(
        functools.partial(per_device, mesh.shape["dp"], mesh.shape["cent"]),
        mesh=mesh,
        in_specs=placed,
        out_specs=(P("cent", None), P(("dp", "cent"))),
        check_vma=False,
    )
```

```python
import functools

import jax
import jax.numpy as jnp
from jax import lax
from jax.experimental import pallas as pl
from jax.experimental.pallas import tpu as pltpu
from jax.sharding import PartitionSpec as P

F32 = jnp.float32
BF16 = jnp.bfloat16
LANES = 128
CHUNK = 128
PIECES = 2


def dot_nt(a, b):
    return lax.dot_general(a, b, (((1,), (1,)), ((), ())), preferred_element_type=F32)


def iota(shape, dim):
    return lax.broadcasted_iota(jnp.int32, shape, dim)


def remote(src, dst, send, recv, where):
    return pltpu.make_async_remote_copy(
        src_ref=src, dst_ref=dst, send_sem=send, recv_sem=recv,
        device_id=where, device_id_type=pl.DeviceIdType.MESH)


def kernel(ndp, ncent, wa, points_ref, assign_ref, cent_ref, counts_ref,
           fresh_ref, best_ref,
           pts, labs, keys, acc, sel, sellab, merged, rounded, outbest, inbest,
           pts_send, pts_recv, lab_send, lab_recv, sel_send, sel_recv,
           sl_send, sl_recv, best_send, best_recv, loc):
    pdev, width = points_ref.shape
    kdev = cent_ref.shape[0]
    wide = sellab.shape[2]
    wb = ncent // (2 * wa)
    me = lax.axis_index("cent")
    mydp = lax.axis_index("dp")
    core = lax.rem(me, 2)
    b = lax.rem(me // 2, wb)
    a = me // (2 * wb)

    fetch = pltpu.make_async_copy(cent_ref, merged, loc.at[0])
    fetch.start()

    def block(s):
        return pts.at[pl.ds(pl.multiple_of(s * pdev, 16), pdev), :]

    own = pltpu.make_async_copy(points_ref, block(me), loc.at[1])
    own.start()

    barrier = pltpu.get_barrier_semaphore()
    for o in range(1, ncent):
        pl.semaphore_signal(barrier, inc=1, device_id={"cent": lax.rem(me + o, ncent)},
                            device_id_type=pl.DeviceIdType.MESH)
    for o in range(1, ndp):
        pl.semaphore_signal(barrier, inc=1, device_id={"dp": lax.rem(mydp + o, ndp)},
                            device_id_type=pl.DeviceIdType.MESH)
    labs[me] = jnp.full((1, LANES), -1, jnp.int32)
    labs[me, 0:1, 0:pdev] = assign_ref[...]
    own.wait()
    pl.semaphore_wait(barrier, ncent + ndp - 2)

    def index(a_, b_, c_):
        return (a_ * wb + b_) * 2 + c_

    if wa == 4:
        half = a // 2
        others = [1 - a + 4 * half, 2 - half, 3 - 3 * half]
    else:
        others = [lax.rem(a + o, wa) for o in range(1, wa)]
    bothers = [lax.rem(b + o, wb) for o in range(1, wb)]
    sent = []

    piece = width // PIECES

    def part(s, q):
        rows = pl.ds(pl.multiple_of(s * pdev, 16), pdev)
        return block(s) if q is None else pts.at[rows, q * piece:(q + 1) * piece]

    def send(s, to, q, when=None):
        i = len(sent)

        def copy():
            return remote(part(s, q), part(s, q), pts_send.at[i], pts_recv.at[s, q or 0], {"cent": to})

        sent.append((when, copy))
        if when is None:
            copy().start()
        else:
            pl.when(when)(lambda: copy().start())

    def arrive(s, q=None):
        remote(part(s, q), part(s, q), pts_send.at[0], pts_recv.at[s, q or 0], {"cent": me}).wait_recv()

    for q in range(PIECES):
        send(me, index(a - 1, b, core), q, a > 0)
        send(me, index(a + 1, b, core), q, a < wa - 1)
        for b_ in bothers:
            send(me, index(a, b_, core), q)
    send(me, index(a, b, 1 - core), None)
    labcopies = []
    for o in range(1, ncent):
        to = lax.rem(me + o, ncent)
        c = remote(labs.at[me], labs.at[me], lab_send.at[o], lab_recv.at[me], {"cent": to})
        c.start()
        labcopies.append(c)

    eye = iota((CHUNK, CHUNK), 0) == iota((CHUNK, CHUNK), 1)
    fetch.wait()
    for j in range(kdev // CHUNK):
        rows = pl.ds(j * CHUNK, CHUNK)
        line = counts_ref[:, j * CHUNK:(j + 1) * CHUNK].astype(F32)
        column = jnp.sum(jnp.where(eye, line, 0.0), axis=1, keepdims=True)
        merged[rows, :] = merged[rows, :] * column

    for k in range(1, wa):
        for q in range(PIECES):
            for way in (1, -1):
                origin = a + way * k
                valid = (origin < wa) if way > 0 else (origin >= 0)
                onward = (a > 0) if way > 0 else (a < wa - 1)
                s = index(origin, b, core)
                pl.when(valid)(lambda s=s, q=q: arrive(s, q))
                if k < wa - 1:
                    send(s, index(a - way, b, core), q, valid & onward)
                for b_ in bothers:
                    send(s, index(a, b_, core), q, valid)
                if q == PIECES - 1:
                    send(s, index(a, b, 1 - core), None, valid)

    for o in range(1, ncent):
        s = lax.rem(me + o, ncent)
        remote(labs.at[s], labs.at[s], lab_send.at[0], lab_recv.at[s], {"cent": me}).wait_recv()
    local = labs[...].reshape(ncent, LANES) - me * kdev
    mine = (local >= 0) & (local < kdev) & (iota((ncent, LANES), 1) < pdev)
    ones = jnp.where(mine, 1.0, 0.0).astype(BF16)
    upper = jnp.where(iota((LANES, LANES), 0) < iota((LANES, LANES), 1), 1.0, 0.0).astype(BF16)
    lower = jnp.where(iota((ncent, ncent), 1) < iota((ncent, ncent), 0), 1.0, 0.0).astype(BF16)
    within = jnp.dot(ones, upper, preferred_element_type=F32)
    before = jnp.sum(jnp.dot(lower, ones, preferred_element_type=F32), axis=1, keepdims=True)
    keys[...] = jnp.where(mine, within + before, -1.0)

    slot = iota((pdev, LANES), 0).astype(F32)
    localf = jnp.where(mine, local + 1, 0).astype(F32)
    keyv = keys[...]
    total = jnp.zeros((pdev, LANES), F32)
    for s in range(ncent):
        total += jnp.where(slot == keyv[s:s + 1, :], localf[s:s + 1, :], 0.0)
    labcol = jnp.sum(total, axis=1, keepdims=True)
    place = iota((pdev, wide), 1) == iota((pdev, wide), 0) + mydp * pdev
    sellab[mydp] = jnp.sum(jnp.where(place, labcol, 0.0), axis=0, keepdims=True)
    slcopies = []
    for o in range(1, ndp):
        to = lax.rem(mydp + o, ndp)
        c = remote(sellab.at[mydp], sellab.at[mydp], sl_send.at[o], sl_recv.at[mydp], {"dp": to})
        c.start()
        slcopies.append(c)
    if sel.shape[0] > ndp * pdev:
        sel[ndp * pdev:, :] = jnp.zeros((sel.shape[0] - ndp * pdev, width), BF16)

    def pick(s):
        key = keys[pl.ds(s, 1), :]
        choose = jnp.where(slot == key, 1.0, 0.0).astype(BF16)[:, :pdev]
        return jnp.dot(choose, block(s)[...], preferred_element_type=F32)

    acc[...] = pick(me)
    for a_ in others:
        acc[...] += pick(index(a_, b, core))
    arrive(index(a, b, 1 - core))
    acc[...] += pick(index(a, b, 1 - core))
    for a_ in others:
        s = index(a_, b, 1 - core)
        arrive(s)
        acc[...] += pick(s)
    for a_ in [a] + others:
        for b_ in bothers:
            s = index(a_, b_, core)
            for q in range(PIECES):
                arrive(s, q)
            send(s, index(a, b, 1 - core), None)
            acc[...] += pick(s)
    for a_ in [a] + others:
        for b_ in bothers:
            s = index(a_, b_, 1 - core)
            arrive(s)
            acc[...] += pick(s)

    def selrows(d):
        return sel.at[pl.ds(pl.multiple_of(d * pdev, 16), pdev), :]

    selrows(mydp)[...] = acc[...].astype(BF16)
    selcopies = []
    for o in range(1, ndp):
        to = lax.rem(mydp + o, ndp)
        c = remote(selrows(mydp), selrows(mydp), sel_send.at[o], sel_recv.at[mydp], {"dp": to})
        c.start()
        selcopies.append(c)
    for o in range(1, ndp):
        d = lax.rem(mydp + o, ndp)
        remote(sellab.at[d], sellab.at[d], sl_send.at[0], sl_recv.at[d], {"dp": mydp}).wait_recv()
        remote(selrows(d), selrows(d), sel_send.at[0], sel_recv.at[d], {"dp": mydp}).wait_recv()

    labrow = jnp.sum(sellab[...].reshape(ndp, wide), axis=0, keepdims=True) - 1.0
    for j in range(kdev // CHUNK):
        rows = pl.ds(j * CHUNK, CHUNK)
        ids = (iota((CHUNK, wide), 0) + j * CHUNK).astype(F32)
        onehot = jnp.where(ids == labrow, 1.0, 0.0).astype(BF16)
        value = merged[rows, :] + jnp.dot(onehot, sel[...], preferred_element_type=F32)
        value = value * lax.rsqrt(jnp.mean(value * value, axis=1, keepdims=True) + 1e-05)
        fresh_ref[rows, :] = value
        rounded[rows, :] = value.astype(BF16)

    npts = ncent * pdev
    step = 256 if npts % 256 == 0 else 128
    parts = []
    for t in range(npts // step):
        scores = dot_nt(rounded[...], pts[t * step:(t + 1) * step, :])
        parts.append(jnp.max(scores, axis=0, keepdims=True))
    line = jnp.concatenate(parts, axis=1)
    for s in range(ncent):
        turned = pltpu.roll(line, (npts - s * pdev) % npts, 1) if s else line
        outbest[s] = turned[:, :LANES]
    bestcopies = []
    for o in range(1, ncent):
        to = lax.rem(me + o, ncent)
        c = remote(outbest.at[to], inbest.at[me], best_send.at[o], best_recv.at[me], {"cent": to})
        c.start()
        bestcopies.append(c)
    inbest[me] = outbest[me]

    values = block(me)[...].astype(F32)
    square = jnp.mean(values * values, axis=1, keepdims=True)
    diag = iota((pdev, pdev), 0) == iota((pdev, pdev), 1)
    square = jnp.sum(jnp.where(diag, square, 0.0), axis=0, keepdims=True)
    scale = width * jnp.sqrt(square + 1e-06)

    for when, copy in sent:
        if when is None:
            copy().wait_send()
        else:
            pl.when(when)(lambda copy=copy: copy().wait_send())
    for c in labcopies + slcopies + selcopies:
        c.wait_send()
    for o in range(1, ncent):
        s = lax.rem(me + o, ncent)
        remote(outbest.at[s], inbest.at[s], best_send.at[0], best_recv.at[s], {"cent": me}).wait_recv()
    top = jnp.max(inbest[...].reshape(ncent, LANES), axis=0, keepdims=True)
    best_ref[...] = top[:, :pdev] / scale
    for c in bestcopies:
        c.wait_send()


def per_device(ndp, ncent, points, assign, centroids, counts):
    kdev, width = centroids.shape
    pdev = points.shape[0]
    wa = 4
    wb = ncent // (2 * wa)
    wide = -(-ndp * pdev // LANES) * LANES
    nsend = PIECES * (wb + 2 + 2 * (wa - 1) * (wb + 1)) + wa * wb
    vmem = pl.BlockSpec(memory_space=pltpu.VMEM)
    hbm = pl.BlockSpec(memory_space=pltpu.MemorySpace.HBM)
    dma = pltpu.SemaphoreType.DMA
    fresh, best = pl.pallas_call(
        functools.partial(kernel, ndp, ncent, wa),
        out_shape=(pltpu.MemorySpace.VMEM((kdev, width), F32), jax.ShapeDtypeStruct((1, pdev), F32)),
        in_specs=[hbm, vmem, hbm, vmem],
        out_specs=(vmem, vmem),
        scratch_shapes=[
            pltpu.VMEM((ncent * pdev, width), BF16),
            pltpu.VMEM((ncent, 1, LANES), jnp.int32),
            pltpu.VMEM((ncent, LANES), F32),
            pltpu.VMEM((pdev, width), F32),
            pltpu.VMEM((wide, width), BF16),
            pltpu.VMEM((ndp, 1, wide), F32),
            pltpu.VMEM((kdev, width), F32),
            pltpu.VMEM((kdev, width), BF16),
            pltpu.VMEM((ncent, 1, LANES), F32),
            pltpu.VMEM((ncent, 1, LANES), F32),
            dma((nsend,)), dma((ncent, PIECES)), dma((ncent,)), dma((ncent,)),
            dma((ndp,)), dma((ndp,)), dma((ndp,)), dma((ndp,)),
            dma((ncent,)), dma((ncent,)), dma((2,)),
        ],
        compiler_params=pltpu.CompilerParams(
            collective_id=0, has_side_effects=True, vmem_limit_bytes=60 * 2**20),
    )(points, assign.reshape(1, pdev), centroids, counts.reshape(1, kdev))
    return fresh, best.reshape(pdev)


def solution(mesh):
    placed = (P(("dp", "cent"), None), P(("dp", "cent")), P("cent", None), P("cent"))
    return jax.shard_map(
        functools.partial(per_device, mesh.shape["dp"], mesh.shape["cent"]),
        mesh=mesh,
        in_specs=placed,
        out_specs=(P("cent", None), P(("dp", "cent"))),
        check_vma=False,
    )
```
